32 devices in a mesh: grp: 2 (over x), row: 8 (over z, y), col: 2 (over core).
Axes of the slice: x: 2, y: 2, z: 4, core: 2. Of those that a mesh axis runs over, the one named last changes fastest.
Arguments:
- state: float32 [4, 256, 4096], P(None, ('grp', 'row', 'col')), parts along dimension 1, may hold values from -1.5 to 4.5, as said below
- bed_slope: float32 [2, 256, 4096], P(None, ('grp', 'row', 'col')), parts along dimension 1, may hold values from -1.2 to 1.2
- terrain: int32 [256, 4096], P(('grp', 'row', 'col')), parts along dimension 0, may hold values from 0 to 3
- wet_mask: int32 [256, 4096], P(('grp', 'row', 'col')), parts along dimension 0, may hold values 0 or 1
- state_cotangent: float32 [4, 256, 4096], P(None, ('grp', 'row', 'col')), parts along dimension 1, may hold values from -12 to 12
- roughness: float32 [4], replicated, may hold values from 0.5 to 2
- first_weight: float32 [32, 6], replicated, may hold values from -2.5 to 2.5
- second_weight: float32 [32, 32], replicated, may hold values from -1 to 1
- third_weight: float32 [32, 32], replicated, may hold values from -1 to 1
- output_weight: float32 [3, 32], replicated, may hold values from -1 to 1
- biases: float32 [3, 32], replicated, may hold values from -2 to 2
Outputs:
- final_state: float32 [4, 256, 4096], P(None, ('grp', 'row', 'col')), parts along dimension 1
- state_grad: float32 [4, 256, 4096], P(None, ('grp', 'row', 'col')), parts along dimension 1
- first_grad: float32 [64, 6], P('grp'), parts along dimension 0
- second_grad: float32 [64, 32], P('grp'), parts along dimension 0
- third_grad: float32 [64, 32], P('grp'), parts along dimension 0
- output_grad: float32 [6, 32], P('grp'), parts along dimension 0
- bias_grad: float32 [6, 32], P('grp'), parts along dimension 0
The draws below stay inside these ranges and needn't reach their ends.
There are 2 independent parts, one for each index of `grp`. The reference program is written for one: setup_inputs(seed, part) draws one part's arguments, and reference() takes and returns one part's arrays. A program takes and returns all parts, laid end to end along the dimension named above; an argument that names none is the same for every part. Nothing has to cross between parts.
Inputs may be any that keep to these rules, and one draw needn't show every extreme that they name: `state`: depths are positive.
All inputs are finite; a program needn't handle non-finite values. No bound on the sum of `wet_mask` on one device may be relied on, other than what follows from the above.
Results may differ from the reference program's by a relative error of at most 0.00013.
Values sent between devices are 32-bit elements; how exact they have to be, the bound alone decides.
A program may use at most 128 MiB of HBM per device.

```python
import math
import jax
import jax.numpy as jnp
from jax import lax

NC = 4096
STEPS = 6
HID = 32
FEAT = 6
OUTS = 3
CLASSES = 4
NR = 128


def draw_state(key, part):
    key = jax.random.fold_in(key, 11)
    key_depth, key_flow, key_water = jax.random.split(key, 3)
    row_index = jnp.arange(NR, dtype=jnp.float32)[:, None]
    rising = 1.0 + 2.0 * row_index / max(NR - 1, 1)
    uniform_draw = jax.random.uniform(key_depth, (NR, NC), jnp.float32)
    depth = (0.5 + uniform_draw) * rising
    flows = 0.5 * jnp.clip(jax.random.normal(key_flow, (2, NR, NC), jnp.float32), -3.0, 3.0)
    water = 0.2 + 0.8 * jax.random.uniform(key_water, (NR, NC), jnp.float32)
    return jnp.concatenate((depth[None], flows, water[None]), axis=0)


def draw_state_cotangent(key, part):
    key = jax.random.fold_in(key, 12)
    key_own = jax.random.fold_in(key, 1)
    row_index = jnp.arange(NR, dtype=jnp.float32)[:, None]
    rising = 1.0 + 2.0 * row_index / max(NR - 1, 1)
    values = jnp.clip(jax.random.normal(key_own, (4, NR, NC), jnp.float32), -4.0, 4.0) * rising
    return values


def place_ends(result, key, smallest, largest):
    longest = result.shape.index(max(result.shape))
    spots = []
    for shift in (0, 1):
        where = [jax.random.randint(jax.random.fold_in(key, axis), (), 0, length) for axis, length in enumerate(result.shape)]
        where[longest] = (where[longest] + shift) % result.shape[longest]
        spots.append(tuple(where))
    return result.at[spots[0]].set(smallest).at[spots[1]].set(largest)


def level_of(own_key, extent, cuts, least, largest):
    loudness, own = 1.0, jax.random.fold_in(own_key, 6)
    for position, parts in cuts:
        draws = jnp.exp(jax.random.uniform(jax.random.fold_in(own, position), (parts,), jnp.float32, least / len(cuts), largest / len(cuts)))
        loudness = loudness * jnp.repeat(draws, extent[position] // parts).reshape([-1 if axis == position else 1 for axis in range(len(extent))])
    return loudness


def noise(rng, shape, deviation, most, pieces=(), kind=jnp.bfloat16):
    array = jax.random.normal(rng, shape, jnp.float32) * deviation
    if len(pieces) > 0:
        array = level_of(rng, shape, pieces, -0.22, 0.18) * array
    return jnp.clip(array, min=-most, max=most).astype(kind)


def setup_inputs(seed: int = 0, part: int = 0) -> dict:
    key_list = jax.random.split(jax.random.key(seed), 12)
    own_keys = jax.random.split(jax.random.fold_in(key_list[11], part), 12)
    state = draw_state(jax.random.fold_in(jax.random.fold_in(key_list[11], part), 71), part)
    bed_slope = noise(own_keys[1], (2, NR, NC), 0.3, 1.2, ((1, 16),), jnp.float32)
    terrain = place_ends(jax.random.randint(own_keys[2], (NR, NC), 0, CLASSES), jax.random.fold_in(own_keys[2], 1), 0, CLASSES - 1).astype(jnp.int32)
    wet_mask = place_ends((jax.random.randint(own_keys[3], (NR, NC), 0, 4) < 3).astype(jnp.int32), jax.random.fold_in(own_keys[3], 1), 0, 1)
    state_cotangent = draw_state_cotangent(jax.random.fold_in(jax.random.fold_in(key_list[11], part), 71), part)
    roughness = jnp.clip(jnp.exp(jax.random.uniform(key_list[5], (CLASSES,), jnp.float32, math.log(0.5), math.log(2.0))), 0.5, 2.0)
    first_weight = noise(key_list[6], (HID, FEAT), FEAT ** -0.5, 2.5, (), jnp.float32)
    second_weight = noise(key_list[7], (HID, HID), HID ** -0.5, 1.0, (), jnp.float32)
    third_weight = noise(key_list[8], (HID, HID), HID ** -0.5, 1.0, (), jnp.float32)
    output_weight = noise(key_list[9], (OUTS, HID), HID ** -0.5, 1.0, (), jnp.float32)
    biases = noise(key_list[10], (3, HID), 0.5, 2.0, (), jnp.float32)
    return {"state": state, "bed_slope": bed_slope, "terrain": terrain, "wet_mask": wet_mask, "state_cotangent": state_cotangent, "roughness": roughness, "first_weight": first_weight, "second_weight": second_weight, "third_weight": third_weight, "output_weight": output_weight, "biases": biases}


GRAVITY = 2.0
COURANT = 0.5
SMOOTH = 0.2
EXACT = lax.Precision.HIGHEST

def network(features, first_weight, second_weight, third_weight, output_weight, biases):
    hidden = jnp.tanh(jnp.dot(first_weight, features, precision=EXACT, preferred_element_type=jnp.float32) + biases[0][:, None])
    hidden = jnp.tanh(jnp.dot(second_weight, hidden, precision=EXACT, preferred_element_type=jnp.float32) + biases[1][:, None])
    hidden = jnp.tanh(jnp.dot(third_weight, hidden, precision=EXACT, preferred_element_type=jnp.float32) + biases[2][:, None])
    return jnp.dot(output_weight, hidden, precision=EXACT, preferred_element_type=jnp.float32)

def closure(features, weights):
    saved = jax.checkpoint(network)
    mapped = lax.map(lambda row_cells: saved(row_cells, *weights), jnp.moveaxis(features, 1, 0))
    return jnp.moveaxis(mapped, 0, 1)

def cell_roughness(terrain, roughness):
    classes = jnp.arange(roughness.shape[0], dtype=jnp.int32)
    return lax.optimization_barrier(jnp.sum(jnp.where(terrain[None] == classes[:, None, None], roughness[:, None, None], 0.0), axis=0))

def update(padded, bed_slope, rough_cell, wet_float, weights, time_step):
    centre = padded[:, 1:-1, 1:-1]
    eastern = padded[:, 1:-1, 2:]
    western = padded[:, 1:-1, :-2]
    northern = padded[:, 2:, 1:-1]
    southern = padded[:, :-2, 1:-1]
    laplace = eastern + western + northern + southern - 4.0 * centre
    along_x = 0.5 * (eastern - western)
    along_y = 0.5 * (northern - southern)
    drag = closure(jnp.concatenate((centre, bed_slope), axis=0), weights)
    depth = centre[0]
    new_depth = depth - time_step * (along_x[1] + along_y[2]) + SMOOTH * laplace[0]
    new_flow_x = centre[1] - time_step * GRAVITY * depth * (along_x[0] + bed_slope[0]) + SMOOTH * laplace[1] - time_step * rough_cell * wet_float * drag[0]
    new_flow_y = centre[2] - time_step * GRAVITY * depth * (along_y[0] + bed_slope[1]) + SMOOTH * laplace[2] - time_step * rough_cell * wet_float * drag[1]
    new_water = centre[3] + SMOOTH * laplace[3] + time_step * wet_float * drag[2]
    return jnp.stack((new_depth, new_flow_x, new_flow_y, new_water), axis=0)

def reference(state, bed_slope, terrain, wet_mask, state_cotangent, roughness, first_weight, second_weight, third_weight, output_weight, biases):
    rough_cell = cell_roughness(terrain, roughness)
    wet_float = wet_mask.astype(jnp.float32)

    def forward(initial, weights):
        current = initial
        for number in range(STEPS):
            deepest = lax.stop_gradient(jnp.max(current[0]))
            time_step = COURANT / jnp.sqrt(GRAVITY * deepest)
            padded = jnp.pad(current, ((0, 0), (1, 1), (1, 1)))
            current = update(padded, bed_slope, rough_cell, wet_float, weights, time_step)
        return current
    weights = (first_weight, second_weight, third_weight, output_weight, biases)
    final_state, pullback = jax.vjp(forward, state, weights)
    state_grad, grads = pullback(state_cotangent)
    grad_scale = 1.0 / math.sqrt(NR * NC)
    return (final_state, state_grad, grads[0] * grad_scale, grads[1] * grad_scale, grads[2] * grad_scale, grads[3] * grad_scale, grads[4] * grad_scale)
```

```python
import functools
import math

import jax
import jax.numpy as jnp
from jax import lax
from jax.experimental import pallas as pl
from jax.experimental.pallas import tpu as pltpu
from jax.sharding import PartitionSpec as P

STEPS = 6
GRAVITY = 2.0
COURANT = 0.5
SMOOTH = 0.2
HID = 32
ROWS = 8
WIDE = HID * ROWS
CHUNK = 512
F32, BF16 = jnp.float32, jnp.bfloat16


def dot(a, b, ca=1, cb=0):
    return lax.dot_general(a, b, (((ca,), (cb,)), ((), ())), preferred_element_type=F32)


def split(x):
    hi = x.astype(BF16)
    lo = (x - hi.astype(F32)).astype(BF16)
    return hi, lo


def split3(x):
    hi = x.astype(BF16)
    rest = x - hi.astype(F32)
    mid = rest.astype(BF16)
    return hi, mid, (rest - mid.astype(F32)).astype(BF16)


def iota(shape, dim):
    return lax.broadcasted_iota(jnp.int32, shape, dim)


def wrapped(index, period):
    return index - period * (index >= period) - period * (index >= 2 * period)


def spread(count, period, transposed=False):
    shape = (HID, count) if transposed else (count, HID)
    stacked, unit = (1, 0) if transposed else (0, 1)
    return ((wrapped(iota(shape, stacked), period) >> 3) == iota(shape, unit)).astype(F32).astype(BF16)


def same_row(shape):
    return (iota(shape, 0) & 7) == (iota(shape, 1) & 7)


def widened(small, rows, cols, transposed, period):
    keep = same_row((rows, cols))
    left, right = spread(rows, rows), spread(cols, period)
    result = []
    for part in split(small):
        half = dot(left, part, 1, 1 if transposed else 0).astype(BF16)
        full = dot(half, right, 1, 1)
        result.append(jnp.where(keep, full, 0.0))
    return result


def stacked3(small, rows, unit, transposed):
    hi, lo = widened(small, rows, 3 * unit, transposed, unit)
    col = iota(hi.shape, 1)
    return jnp.where((col >= unit) & (col < 2 * unit), lo, hi).astype(BF16)


def shifted(x, before, after):
    row, col = iota(x.shape, 0), iota(x.shape, 1)
    length = x.shape[1]
    north = jnp.where(row == ROWS - 1, after, pltpu.roll(x, ROWS - 1, 0))
    south = jnp.where(row == 0, before, pltpu.roll(x, 1, 0))
    east = jnp.where(col == length - 1, 0.0, pltpu.roll(x, length - 1, 1))
    west = jnp.where(col == 0, 0.0, pltpu.roll(x, 1, 1))
    return east, west, north, south


def kernel(
    n, ncol, cols,
    state, bed, terrain, wet_mask, cotangent, params, roughness,
    final, adjoint, grads,
    traj, lam, drag, dfeat, rough_wet, wet, steps_dt,
    w1, w2, w3, w4, w2t, w3t, w4t, w1t, bias,
    g1, g2, g3, g4, gb,
    edge_f, halo_f, edge_b, halo_b, peak, peaks, own_grad, all_grads,
    edge_ss, edge_rs, peak_ss, peak_rs, grad_ss, grad_rs,
):
    me = lax.axis_index("row") * ncol + lax.axis_index("col")

    def device(p):
        return {"row": p // ncol, "col": p % ncol}

    def peer(i):
        return lax.rem(me + i, n)

    before_id, after_id = peer(n - 1), peer(1)
    barrier = pltpu.get_barrier_semaphore()

    @pl.loop(1, n)
    def _(i):
        pl.semaphore_signal(barrier, inc=1, device_id=device(peer(i)), device_id_type=pl.DeviceIdType.MESH)

    m1, m2, m3, m4 = (params[32 * i : 32 * i + 32, :] for i in range(4))
    w1[...] = stacked3(m1, WIDE, 48, False)
    w4t[...] = stacked3(m4, WIDE, 32, True)
    for ref, small, rows, transposed in (
        (w2, m2, WIDE, False), (w3, m3, WIDE, False), (w4, m4, 32, False),
        (w2t, m2, WIDE, True), (w3t, m3, WIDE, True), (w1t, m1, 32, True),
    ):
        for k, part in enumerate(widened(small, rows, WIDE, transposed, WIDE)):
            ref[k] = part.astype(BF16)
    for layer in range(3):
        line = jnp.broadcast_to(params[128 + layer : 129 + layer, :], (128, HID))
        bias[layer] = sum(dot(spread(WIDE, WIDE), part, 1, 1) for part in split3(line))
    for ref in (g1, g2, g3, g4, gb):
        ref[...] = jnp.zeros_like(ref)
    kinds = terrain[...]
    rough = jnp.zeros(kinds.shape, F32)
    for k in range(roughness.shape[0]):
        rough = jnp.where(kinds == k, roughness[k], rough)
    wet[...] = wet_mask[...].astype(F32)
    rough_wet[...] = rough * wet[...]
    traj[0] = state[...]
    lam[...] = cotangent[...]

    pl.semaphore_wait(barrier, n - 1)

    def edge_copies(number, step, edge, halo):
        return [
            pltpu.make_async_remote_copy(
                src_ref=edge.at[step, side], dst_ref=halo.at[step, 1 - side],
                send_sem=edge_ss.at[number, side], recv_sem=edge_rs.at[number, 1 - side],
                device_id=device(target), device_id_type=pl.DeviceIdType.MESH,
            )
            for side, target in ((0, before_id), (1, after_id))
        ]

    def arriving(number, step, edge, halo):
        return [
            pltpu.make_async_remote_copy(
                src_ref=edge.at[step, 1 - side], dst_ref=halo.at[step, side],
                send_sem=edge_ss.at[number, 1 - side], recv_sem=edge_rs.at[number, side],
                device_id=device(before_id), device_id_type=pl.DeviceIdType.MESH,
            )
            for side in (0, 1)
        ]

    def send_edges(number, step, edge, halo, field):
        for f in range(4):
            edge[step, 0, f : f + 1, :] = field(f, 0)
            edge[step, 1, f : f + 1, :] = field(f, ROWS - 1)
        for copy in edge_copies(number, step, edge, halo):
            copy.start()

    def take_edges(number, step, edge, halo):
        for copy in arriving(number, step, edge, halo):
            copy.wait_recv()
        for copy in edge_copies(number, step, edge, halo):
            copy.wait_send()

    def peak_copy(step, i):
        return pltpu.make_async_remote_copy(
            src_ref=peak.at[step], dst_ref=peaks.at[step, me],
            send_sem=peak_ss.at[i], recv_sem=peak_rs.at[step, me],
            device_id=device(peer(i)), device_id_type=pl.DeviceIdType.MESH,
        )

    def peak_arrival(step, i):
        return pltpu.make_async_remote_copy(
            src_ref=peak.at[step], dst_ref=peaks.at[step, peer(i)],
            send_sem=peak_ss.at[i], recv_sem=peak_rs.at[step, peer(i)],
            device_id=device(peer(i)), device_id_type=pl.DeviceIdType.MESH,
        )

    has_before = jnp.where(me > 0, 1.0, 0.0).astype(F32)
    has_after = jnp.where(me < n - 1, 1.0, 0.0).astype(F32)

    def across(tile, width):
        return jnp.concatenate([tile] * (width // 128), axis=1)

    def layer(weight, hi, lo):
        return dot(weight[0], hi) + dot(weight[0], lo) + dot(weight[1], hi)

    def hidden(step, at):
        x = jnp.concatenate([traj[step, :, at], bed[:, at]], axis=0)
        xhi, xlo = split(x)
        a1 = jnp.tanh(dot(w1[...], jnp.concatenate([xhi, xhi, xlo], axis=0)) + across(bias[0], CHUNK))
        s1 = split(a1)
        a2 = jnp.tanh(layer(w2, *s1) + across(bias[1], CHUNK))
        s2 = split(a2)
        a3 = jnp.tanh(layer(w3, *s2) + across(bias[2], CHUNK))
        return (xhi, xlo), a1, s1, a2, s2, a3, split(a3)

    def forward(step, _):
        send_edges(step, step, edge_f, halo_f, lambda f, r: traj[step, 8 * f + r : 8 * f + r + 1, :])
        depth = traj[step, 0:ROWS, :]
        deepest = depth[:, 0:128]
        for k in range(1, cols // 128):
            deepest = jnp.maximum(deepest, depth[:, 128 * k : 128 * k + 128])
        peak[step] = deepest
        peaks[step, me] = deepest

        @pl.loop(1, n)
        def _(i):
            peak_copy(step, i).start()

        @pl.loop(0, cols // CHUNK)
        def _(c):
            at = pl.ds(pl.multiple_of(c * CHUNK, CHUNK), CHUNK)
            s3 = hidden(step, at)[-1]
            drag[:, at] = layer(w4, *s3)

        @pl.loop(1, n)
        def _(i):
            peak_arrival(step, i).wait_recv()
            peak_copy(step, i).wait_send()

        largest = jnp.max(jnp.max(peaks[step], axis=0))
        tile = COURANT / jnp.sqrt(GRAVITY * jnp.full((ROWS, 128), largest, F32))
        steps_dt[step] = tile
        dt = across(tile, cols)
        take_edges(step, step, edge_f, halo_f)
        fields = [traj[step, 8 * f : 8 * f + 8, :] for f in range(4)]
        near = [
            shifted(
                fields[f],
                halo_f[step, 0, f : f + 1, :] * has_before,
                halo_f[step, 1, f : f + 1, :] * has_after,
            )
            for f in range(4)
        ]
        smooth = [SMOOTH * (e + w + n_ + s - 4.0 * fields[f]) for f, (e, w, n_, s) in enumerate(near)]

        def ddx(f):
            return 0.5 * (near[f][0] - near[f][1])

        def ddy(f):
            return 0.5 * (near[f][2] - near[f][3])

        depth = fields[0]
        traj[step + 1, 0:8, :] = depth - dt * (ddx(1) + ddy(2)) + smooth[0]
        traj[step + 1, 8:16, :] = (
            fields[1] - dt * GRAVITY * depth * (ddx(0) + bed[0:8, :]) + smooth[1] - dt * rough_wet[...] * drag[0:8, :]
        )
        traj[step + 1, 16:24, :] = (
            fields[2] - dt * GRAVITY * depth * (ddy(0) + bed[8:16, :]) + smooth[2] - dt * rough_wet[...] * drag[8:16, :]
        )
        traj[step + 1, 24:32, :] = fields[3] + smooth[3] + dt * wet[...] * drag[16:24, :]
        return 0

    lax.fori_loop(0, STEPS, forward, 0)
    final[...] = traj[STEPS]

    def backward(back, _):
        step = STEPS - 1 - back
        number = STEPS + step
        send_edges(number, step, edge_b, halo_b, lambda f, r: lam[8 * f + r : 8 * f + r + 1, :])
        tile = steps_dt[step]

        @pl.loop(0, cols // CHUNK)
        def _(c):
            at = pl.ds(pl.multiple_of(c * CHUNK, CHUNK), CHUNK)
            dt = across(tile, CHUNK)
            pull = -dt * rough_wet[:, at]
            g = jnp.concatenate(
                [pull * lam[8:16, at], pull * lam[16:24, at], dt * wet[:, at] * lam[24:32, at], jnp.zeros((8, CHUNK), F32)],
                axis=0,
            )
            ghi, glo = split(g)
            (xhi, xlo), a1, s1, a2, s2, a3, s3 = hidden(step, at)
            d3 = dot(w4t[...], jnp.concatenate([ghi, ghi, glo], axis=0)) * (1.0 - a3 * a3)
            t3 = split(d3)
            d2 = layer(w3t, *t3) * (1.0 - a2 * a2)
            t2 = split(d2)
            d1 = layer(w2t, *t2) * (1.0 - a1 * a1)
            t1 = split(d1)
            dfeat[:, at] = layer(w1t, *t1)
            both_g = jnp.concatenate([ghi, glo], axis=0)
            both_x = jnp.concatenate([xhi, xlo], axis=0)
            g4[...] += dot(both_g, s3[0], 1, 1) + dot(both_g, s3[1], 1, 1)
            g3[...] += dot(t3[0], s2[0], 1, 1) + dot(t3[0], s2[1], 1, 1) + dot(t3[1], s2[0], 1, 1)
            g2[...] += dot(t2[0], s1[0], 1, 1) + dot(t2[0], s1[1], 1, 1) + dot(t2[1], s1[0], 1, 1)
            g1[...] += dot(t1[0], both_x, 1, 1) + dot(t1[1], both_x, 1, 1)
            for k, d in enumerate((d1, d2, d3)):
                total = d[:, 0:128]
                for j in range(1, CHUNK // 128):
                    total = total + d[:, 128 * j : 128 * j + 128]
                gb[k] += total

        dt = across(tile, cols)
        take_edges(number, step, edge_b, halo_b)
        lams = [lam[8 * f : 8 * f + 8, :] for f in range(4)]
        above = [halo_b[step, 0, f : f + 1, :] * has_before for f in range(4)]
        below = [halo_b[step, 1, f : f + 1, :] * has_after for f in range(4)]
        near = [shifted(lams[f], above[f], below[f]) for f in range(4)]
        smooth = [SMOOTH * (e + w + n_ + s - 4.0 * lams[f]) for f, (e, w, n_, s) in enumerate(near)]
        depth = traj[step, 0:8, :]
        depth_above = halo_f[step, 0, 0:1, :] * has_before
        depth_below = halo_f[step, 1, 0:1, :] * has_after
        e, w, n_, s = shifted(depth, depth_above, depth_below)
        slope_x = 0.5 * (e - w) + bed[0:8, :]
        slope_y = 0.5 * (n_ - s) + bed[8:16, :]
        px_e, px_w, _, _ = shifted(depth * lams[1], depth_above, depth_below)
        _, _, py_n, py_s = shifted(depth * lams[2], depth_above * above[2], depth_below * below[2])
        push = 0.5 * (px_e - px_w + py_n - py_s) - slope_x * lams[1] - slope_y * lams[2]
        lam[0:8, :] = lams[0] + smooth[0] + dt * GRAVITY * push + dfeat[0:8, :]
        lam[8:16, :] = lams[1] + smooth[1] + dt * 0.5 * (near[0][0] - near[0][1]) + dfeat[8:16, :]
        lam[16:24, :] = lams[2] + smooth[2] + dt * 0.5 * (near[0][2] - near[0][3]) + dfeat[16:24, :]
        lam[24:32, :] = lams[3] + smooth[3] + dfeat[24:32, :]
        return 0

    lax.fori_loop(0, STEPS, backward, 0)
    adjoint[...] = lam[...]

    def place(count, period, offset):
        shape = (count, 128)
        return ((wrapped(iota(shape, 0), period) >> 3) + offset == iota(shape, 1)).astype(F32).astype(BF16)

    def collapsed(total, period, col_period, offset):
        rows, width = total.shape
        total = jnp.where(same_row(total.shape), total, 0.0)
        gather = spread(rows, period, transposed=True)
        half = sum(dot(gather, part) for part in split3(total))
        put = place(width, col_period, offset)
        return sum(dot(part, put) for part in split3(half))

    packed = collapsed(g1[...], WIDE, 48, 0)
    packed += collapsed(g2[...], WIDE, WIDE, 32)
    packed += collapsed(g3[...], WIDE, WIDE, 64)
    packed += collapsed(g4[...], 32, WIDE, 96)
    for k in range(3):
        pick = (iota((HID, 128), 0) == 8 + k).astype(F32).astype(BF16)
        half = sum(dot(pick, part, 1, 1) for part in split3(gb[k]))
        packed += sum(dot(part, place(WIDE, WIDE, 96)) for part in split3(half))
    own_grad[...] = packed
    all_grads[me] = packed

    def grad_copy(i):
        return pltpu.make_async_remote_copy(
            src_ref=own_grad, dst_ref=all_grads.at[me],
            send_sem=grad_ss.at[i], recv_sem=grad_rs.at[me],
            device_id=device(peer(i)), device_id_type=pl.DeviceIdType.MESH,
        )

    def grad_arrival(i):
        return pltpu.make_async_remote_copy(
            src_ref=own_grad, dst_ref=all_grads.at[peer(i)],
            send_sem=grad_ss.at[i], recv_sem=grad_rs.at[peer(i)],
            device_id=device(peer(i)), device_id_type=pl.DeviceIdType.MESH,
        )

    @pl.loop(1, n)
    def _(i):
        grad_copy(i).start()

    @pl.loop(1, n)
    def _(i):
        grad_arrival(i).wait_recv()
        grad_copy(i).wait_send()

    grads[...] = jnp.sum(all_grads[...], axis=0) * (1.0 / math.sqrt(ROWS * cols * n))


def shards(
    state, bed_slope, terrain, wet_mask, state_cotangent, roughness,
    first_weight, second_weight, third_weight, output_weight, biases,
):
    nrow, ncol = lax.axis_size("row"), lax.axis_size("col")
    n = nrow * ncol
    cols = state.shape[2]
    assert state.shape[1] == ROWS
    params = jnp.concatenate(
        [
            jnp.pad(first_weight, ((0, 0), (0, HID - first_weight.shape[1]))),
            second_weight,
            third_weight,
            jnp.pad(output_weight, ((0, HID - output_weight.shape[0]), (0, 0))),
            jnp.pad(biases, ((0, 8 - biases.shape[0]), (0, 0))),
        ],
        axis=0,
    )
    vmem = pl.BlockSpec(memory_space=pltpu.VMEM)
    big = (2, WIDE, WIDE)
    final, adjoint, grads = pl.pallas_call(
        functools.partial(kernel, n, ncol, cols),
        out_shape=(
            jax.ShapeDtypeStruct((4 * ROWS, cols), F32),
            jax.ShapeDtypeStruct((4 * ROWS, cols), F32),
            jax.ShapeDtypeStruct((HID, 128), F32),
        ),
        in_specs=[vmem] * 6 + [pl.BlockSpec(memory_space=pltpu.SMEM)],
        out_specs=(vmem, vmem, vmem),
        scratch_shapes=[
            pltpu.VMEM((STEPS + 1, 4 * ROWS, cols), F32),
            pltpu.VMEM((4 * ROWS, cols), F32),
            pltpu.VMEM((4 * ROWS, cols), F32),
            pltpu.VMEM((4 * ROWS, cols), F32),
            pltpu.VMEM((ROWS, cols), F32),
            pltpu.VMEM((ROWS, cols), F32),
            pltpu.VMEM((STEPS, ROWS, 128), F32),
            pltpu.VMEM((WIDE, 144), BF16),
            pltpu.VMEM(big, BF16),
            pltpu.VMEM(big, BF16),
            pltpu.VMEM((2, 32, WIDE), BF16),
            pltpu.VMEM(big, BF16),
            pltpu.VMEM(big, BF16),
            pltpu.VMEM((WIDE, 96), BF16),
            pltpu.VMEM((2, 32, WIDE), BF16),
            pltpu.VMEM((3, WIDE, 128), F32),
            pltpu.VMEM((WIDE, 96), F32),
            pltpu.VMEM((WIDE, WIDE), F32),
            pltpu.VMEM((WIDE, WIDE), F32),
            pltpu.VMEM((64, WIDE), F32),
            pltpu.VMEM((3, WIDE, 128), F32),
            pltpu.VMEM((STEPS, 2, 4, cols), F32),
            pltpu.VMEM((STEPS, 2, 4, cols), F32),
            pltpu.VMEM((STEPS, 2, 4, cols), F32),
            pltpu.VMEM((STEPS, 2, 4, cols), F32),
            pltpu.VMEM((STEPS, ROWS, 128), F32),
            pltpu.VMEM((STEPS, n, ROWS, 128), F32),
            pltpu.VMEM((HID, 128), F32),
            pltpu.VMEM((n, HID, 128), F32),
            pltpu.SemaphoreType.DMA((2 * STEPS, 2)),
            pltpu.SemaphoreType.DMA((2 * STEPS, 2)),
            pltpu.SemaphoreType.DMA((n,)),
            pltpu.SemaphoreType.DMA((STEPS, n)),
            pltpu.SemaphoreType.DMA((n,)),
            pltpu.SemaphoreType.DMA((n,)),
        ],
        compiler_params=pltpu.CompilerParams(
            collective_id=0, has_side_effects=True, vmem_limit_bytes=56 * 1024 * 1024
        ),
    )(
        state.reshape(4 * ROWS, cols),
        bed_slope.reshape(2 * ROWS, cols),
        terrain,
        wet_mask,
        state_cotangent.reshape(4 * ROWS, cols),
        params,
        roughness,
    )
    feat, outs, layers = first_weight.shape[1], output_weight.shape[0], biases.shape[0]
    return (
        final.reshape(state.shape),
        adjoint.reshape(state.shape),
        grads[:, 0:feat],
        grads[:, 32:64],
        grads[:, 64:96],
        grads[0:outs, 96:128],
        grads[8 : 8 + layers, 96:128],
    )


def solution(mesh):
    cells = P(None, ("grp", "row", "col"), None)
    flat = P(("grp", "row", "col"), None)
    in_specs = (cells, cells, flat, flat, cells, P(), P(), P(), P(), P(), P())
    out_specs = (cells, cells) + (P("grp", None),) * 5
    return jax.shard_map(shards, mesh=mesh, in_specs=in_specs, out_specs=out_specs, check_vma=False)
```

```python
import functools
import math

import jax
import jax.numpy as jnp
from jax import lax
from jax.experimental import pallas as pl
from jax.experimental.pallas import tpu as pltpu
from jax.sharding import PartitionSpec as P

STEPS = 6
GRAVITY = 2.0
COURANT = 0.5
SMOOTH = 0.2
HID = 32
ROWS = 8
SLOTS = 4
HALF = HID * SLOTS
WIDE = 2 * HALF
CHUNK = 1024
KEPT = 3
F32, BF16 = jnp.float32, jnp.bfloat16


def dot(a, b, ca=1, cb=0):
    return lax.dot_general(a, b, (((ca,), (cb,)), ((), ())), preferred_element_type=F32)


def split(x):
    hi = x.astype(BF16)
    lo = (x - hi.astype(F32)).astype(BF16)
    return hi, lo


def split3(x):
    hi = x.astype(BF16)
    rest = x - hi.astype(F32)
    mid = rest.astype(BF16)
    return hi, mid, (rest - mid.astype(F32)).astype(BF16)


def iota(shape, dim):
    return lax.broadcasted_iota(jnp.int32, shape, dim)


def wrapped(index, period):
    return index - period * (index >= period) - period * (index >= 2 * period)


def cells(period):
    def where(i):
        inner = wrapped(i, period)
        return inner >> 3, i & 7, (i >= period).astype(jnp.int32) + (i >= 2 * period).astype(jnp.int32)

    return where


def units(half_bit=None):
    def where(i):
        slot = i & 3
        if half_bit is not None:
            slot = slot + 4 * (i >> half_bit)
        return (i & (HALF - 1)) >> 2, slot, (i >> 7) & 1

    return where


def chosen(count, where, transposed=False, lanes=HID, offset=0):
    shape = (lanes, count) if transposed else (count, lanes)
    stacked, unit = (1, 0) if transposed else (0, 1)
    return (where(iota(shape, stacked))[0] + offset == iota(shape, unit)).astype(F32).astype(BF16)


def same_row(shape, row_where, col_where):
    return row_where(iota(shape, 0))[1] == col_where(iota(shape, 1))[1]


def widened(small, shape, row_where, col_where, is_low, transposed):
    left, right = chosen(shape[0], row_where), chosen(shape[1], col_where)
    hi, lo = (
        dot(dot(left, part, 1, 1 if transposed else 0).astype(BF16), right, 1, 1) for part in split(small)
    )
    low = is_low(row_where(iota(shape, 0))[2], col_where(iota(shape, 1))[2])
    full = jnp.where(low, lo, hi)
    return jnp.where(same_row(shape, row_where, col_where), full, 0.0).astype(BF16)


def shifted(x, before, after):
    row, col = iota(x.shape, 0), iota(x.shape, 1)
    length = x.shape[1]
    north = jnp.where(row == ROWS - 1, after, pltpu.roll(x, ROWS - 1, 0))
    south = jnp.where(row == 0, before, pltpu.roll(x, 1, 0))
    east = jnp.where(col == length - 1, 0.0, pltpu.roll(x, length - 1, 1))
    west = jnp.where(col == 0, 0.0, pltpu.roll(x, 1, 1))
    return east, west, north, south


def kernel(
    n, ncol, cols,
    state, bed, terrain, wet_mask, cotangent, params, roughness,
    final, adjoint, grads,
    traj, lam, drag, dfeat, rough_wet, wet, steps_dt,
    w1, w2, w3, w4, w2t, w3t, w4t, w1t, bias, kept,
    g1, g2, g3, g4, gb,
    edge_f, halo_f, edge_b, halo_b, peak, peaks, own_grad, all_grads,
    edge_ss, edge_rs, peak_ss, peak_rs, grad_ss, grad_rs,
):
    me = lax.axis_index("row") * ncol + lax.axis_index("col")

    def device(p):
        return {"row": p // ncol, "col": p % ncol}

    def peer(i):
        return lax.rem(me + i, n)

    before_id, after_id = peer(n - 1), peer(1)
    barrier = pltpu.get_barrier_semaphore()

    @pl.loop(1, n)
    def _(i):
        pl.semaphore_signal(barrier, inc=1, device_id=device(peer(i)), device_id_type=pl.DeviceIdType.MESH)

    m1, m2, m3, m4 = (params[32 * i : 32 * i + 32, :] for i in range(4))
    low_col = lambda r, c: c == 1
    low_row = lambda r, c: r == 1
    w1[...] = widened(m1, (WIDE, 144), units(7), cells(48), low_col, False)
    w4t[...] = widened(m4, (WIDE, 96), units(7), cells(32), low_col, True)
    w4[...] = widened(m4, (64, 2 * WIDE), cells(32), units(8), low_row, False)
    w1t[...] = widened(m1, (64, 2 * WIDE), cells(32), units(8), low_row, True)
    for ref, small, transposed in ((w2, m2, False), (w3, m3, False), (w2t, m2, True), (w3t, m3, True)):
        ref[...] = widened(small, (WIDE, WIDE), units(), units(), low_row, transposed)
    for layer in range(3):
        line = jnp.broadcast_to(params[128 + layer : 129 + layer, :], (128, HID))
        bias[layer] = sum(dot(chosen(HALF, units()), part, 1, 1) for part in split3(line))
    for ref in (g1, g2, g3, g4, gb):
        ref[...] = jnp.zeros_like(ref)
    kinds = terrain[...]
    rough = jnp.zeros(kinds.shape, F32)
    for k in range(roughness.shape[0]):
        rough = jnp.where(kinds == k, roughness[k], rough)
    wet[...] = wet_mask[...].astype(F32)
    rough_wet[...] = rough * wet[...]
    traj[0] = state[...]
    lam[...] = cotangent[...]

    pl.semaphore_wait(barrier, n - 1)

    def edge_copies(number, step, edge, halo):
        return [
            pltpu.make_async_remote_copy(
                src_ref=edge.at[step, side], dst_ref=halo.at[step, 1 - side],
                send_sem=edge_ss.at[number, side], recv_sem=edge_rs.at[number, 1 - side],
                device_id=device(target), device_id_type=pl.DeviceIdType.MESH,
            )
            for side, target in ((0, before_id), (1, after_id))
        ]

    def arriving(number, step, edge, halo):
        return [
            pltpu.make_async_remote_copy(
                src_ref=edge.at[step, 1 - side], dst_ref=halo.at[step, side],
                send_sem=edge_ss.at[number, 1 - side], recv_sem=edge_rs.at[number, side],
                device_id=device(before_id), device_id_type=pl.DeviceIdType.MESH,
            )
            for side in (0, 1)
        ]

    def send_edges(number, step, edge, halo, field):
        for f in range(4):
            edge[step, 0, f : f + 1, :] = field(f, 0)
            edge[step, 1, f : f + 1, :] = field(f, ROWS - 1)
        for copy in edge_copies(number, step, edge, halo):
            copy.start()

    def take_edges(number, step, edge, halo):
        for copy in arriving(number, step, edge, halo):
            copy.wait_recv()
        for copy in edge_copies(number, step, edge, halo):
            copy.wait_send()

    def peak_copy(step, i):
        return pltpu.make_async_remote_copy(
            src_ref=peak.at[step], dst_ref=peaks.at[step, me],
            send_sem=peak_ss.at[i], recv_sem=peak_rs.at[step, me],
            device_id=device(peer(i)), device_id_type=pl.DeviceIdType.MESH,
        )

    def peak_arrival(step, i):
        return pltpu.make_async_remote_copy(
            src_ref=peak.at[step], dst_ref=peaks.at[step, peer(i)],
            send_sem=peak_ss.at[i], recv_sem=peak_rs.at[step, peer(i)],
            device_id=device(peer(i)), device_id_type=pl.DeviceIdType.MESH,
        )

    has_before = jnp.where(me > 0, 1.0, 0.0).astype(F32)
    has_after = jnp.where(me < n - 1, 1.0, 0.0).astype(F32)

    def across(tile, width):
        return jnp.concatenate([tile] * (width // 128), axis=1)

    def folded(y):
        half = y.shape[0] // 2
        return y[:half] + y[half:]

    def side(y):
        return jnp.concatenate([y[:HALF], y[HALF:]], axis=1)

    def under(y):
        return jnp.concatenate([y[:, :CHUNK], y[:, CHUNK:]], axis=0)

    def pair(x):
        return jnp.concatenate(split(x), axis=0)

    def features(step, at):
        return split(jnp.concatenate([traj[step, :, at], bed[:, at]], axis=0))

    def hidden(xhi, xlo):
        wide = 2 * CHUNK
        a1 = jnp.tanh(side(dot(w1[...], jnp.concatenate([xhi, xhi, xlo], axis=0))) + across(bias[0], wide))
        s1 = pair(a1)
        a2 = jnp.tanh(folded(dot(w2[...], s1)) + across(bias[1], wide))
        s2 = pair(a2)
        a3 = jnp.tanh(folded(dot(w3[...], s2)) + across(bias[2], wide))
        return a1, s1, a2, s2, a3, pair(a3)

    def recalled(step, c):
        result = []
        for k in range(3):
            both = kept[step, c, k]
            result += [both[:HALF].astype(F32) + both[HALF:].astype(F32), both]
        return result

    def forward(keep, step, _):
        send_edges(step, step, edge_f, halo_f, lambda f, r: traj[step, 8 * f + r : 8 * f + r + 1, :])
        depth = traj[step, 0:ROWS, :]
        deepest = depth[:, 0:128]
        for k in range(1, cols // 128):
            deepest = jnp.maximum(deepest, depth[:, 128 * k : 128 * k + 128])
        peak[step] = deepest
        peaks[step, me] = deepest

        @pl.loop(1, n)
        def _(i):
            peak_copy(step, i).start()

        @pl.loop(0, cols // CHUNK)
        def _(c):
            at = pl.ds(pl.multiple_of(c * CHUNK, CHUNK), CHUNK)
            _, s1, _, s2, _, s3 = hidden(*features(step, at))
            if keep:
                for k, both in enumerate((s1, s2, s3)):
                    kept[step, c, k] = both
            drag[:, at] = folded(dot(w4[...], under(s3)))

        @pl.loop(1, n)
        def _(i):
            peak_arrival(step, i).wait_recv()
            peak_copy(step, i).wait_send()

        largest = jnp.max(jnp.max(peaks[step], axis=0))
        tile = COURANT / jnp.sqrt(GRAVITY * jnp.full((ROWS, 128), largest, F32))
        steps_dt[step] = tile
        dt = across(tile, cols)
        take_edges(step, step, edge_f, halo_f)
        fields = [traj[step, 8 * f : 8 * f + 8, :] for f in range(4)]
        near = [
            shifted(
                fields[f],
                halo_f[step, 0, f : f + 1, :] * has_before,
                halo_f[step, 1, f : f + 1, :] * has_after,
            )
            for f in range(4)
        ]
        smooth = [SMOOTH * (e + w + n_ + s - 4.0 * fields[f]) for f, (e, w, n_, s) in enumerate(near)]

        def ddx(f):
            return 0.5 * (near[f][0] - near[f][1])

        def ddy(f):
            return 0.5 * (near[f][2] - near[f][3])

        depth = fields[0]
        traj[step + 1, 0:8, :] = depth - dt * (ddx(1) + ddy(2)) + smooth[0]
        traj[step + 1, 8:16, :] = (
            fields[1] - dt * GRAVITY * depth * (ddx(0) + bed[0:8, :]) + smooth[1] - dt * rough_wet[...] * drag[0:8, :]
        )
        traj[step + 1, 16:24, :] = (
            fields[2] - dt * GRAVITY * depth * (ddy(0) + bed[8:16, :]) + smooth[2] - dt * rough_wet[...] * drag[8:16, :]
        )
        traj[step + 1, 24:32, :] = fields[3] + smooth[3] + dt * wet[...] * drag[16:24, :]
        return 0

    lax.fori_loop(0, KEPT, functools.partial(forward, True), 0)
    lax.fori_loop(KEPT, STEPS, functools.partial(forward, False), 0)
    final[...] = traj[STEPS]

    def backward(keep, back, _):
        step = STEPS - 1 - back
        number = STEPS + step
        send_edges(number, step, edge_b, halo_b, lambda f, r: lam[8 * f + r : 8 * f + r + 1, :])
        tile = steps_dt[step]

        @pl.loop(0, cols // CHUNK)
        def _(c):
            at = pl.ds(pl.multiple_of(c * CHUNK, CHUNK), CHUNK)
            dt = across(tile, CHUNK)
            pull = -dt * rough_wet[:, at]
            g = jnp.concatenate(
                [pull * lam[8:16, at], pull * lam[16:24, at], dt * wet[:, at] * lam[24:32, at], jnp.zeros((8, CHUNK), F32)],
                axis=0,
            )
            ghi, glo = split(g)
            xhi, xlo = features(step, at)
            a1, s1, a2, s2, a3, s3 = recalled(step, c) if keep else hidden(xhi, xlo)
            d3 = side(dot(w4t[...], jnp.concatenate([ghi, ghi, glo], axis=0))) * (1.0 - a3 * a3)
            t3 = pair(d3)
            d2 = folded(dot(w3t[...], t3)) * (1.0 - a2 * a2)
            t2 = pair(d2)
            d1 = folded(dot(w2t[...], t2)) * (1.0 - a1 * a1)
            t1 = under(pair(d1))
            dfeat[:, at] = folded(dot(w1t[...], t1))
            g4[...] += dot(jnp.concatenate([ghi, glo], axis=0), under(s3), 1, 1)
            g3[...] += dot(t3, s2, 1, 1)
            g2[...] += dot(t2, s1, 1, 1)
            g1[...] += dot(t1, jnp.concatenate([xhi, xlo], axis=0), 1, 1)
            for k, d in enumerate((d1, d2, d3)):
                total = d[:, 0:128]
                for j in range(1, 2 * CHUNK // 128):
                    total = total + d[:, 128 * j : 128 * j + 128]
                gb[k] += total

        dt = across(tile, cols)
        take_edges(number, step, edge_b, halo_b)
        lams = [lam[8 * f : 8 * f + 8, :] for f in range(4)]
        above = [halo_b[step, 0, f : f + 1, :] * has_before for f in range(4)]
        below = [halo_b[step, 1, f : f + 1, :] * has_after for f in range(4)]
        near = [shifted(lams[f], above[f], below[f]) for f in range(4)]
        smooth = [SMOOTH * (e + w + n_ + s - 4.0 * lams[f]) for f, (e, w, n_, s) in enumerate(near)]
        depth = traj[step, 0:8, :]
        depth_above = halo_f[step, 0, 0:1, :] * has_before
        depth_below = halo_f[step, 1, 0:1, :] * has_after
        e, w, n_, s = shifted(depth, depth_above, depth_below)
        slope_x = 0.5 * (e - w) + bed[0:8, :]
        slope_y = 0.5 * (n_ - s) + bed[8:16, :]
        px_e, px_w, _, _ = shifted(depth * lams[1], depth_above, depth_below)
        _, _, py_n, py_s = shifted(depth * lams[2], depth_above * above[2], depth_below * below[2])
        push = 0.5 * (px_e - px_w + py_n - py_s) - slope_x * lams[1] - slope_y * lams[2]
        lam[0:8, :] = lams[0] + smooth[0] + dt * GRAVITY * push + dfeat[0:8, :]
        lam[8:16, :] = lams[1] + smooth[1] + dt * 0.5 * (near[0][0] - near[0][1]) + dfeat[8:16, :]
        lam[16:24, :] = lams[2] + smooth[2] + dt * 0.5 * (near[0][2] - near[0][3]) + dfeat[16:24, :]
        lam[24:32, :] = lams[3] + smooth[3] + dfeat[24:32, :]
        return 0

    lax.fori_loop(0, STEPS - KEPT, functools.partial(backward, False), 0)
    lax.fori_loop(STEPS - KEPT, STEPS, functools.partial(backward, True), 0)
    adjoint[...] = lam[...]

    def collapsed(total, row_where, col_where, offset):
        total = jnp.where(same_row(total.shape, row_where, col_where), total, 0.0)
        gather = chosen(total.shape[0], row_where, transposed=True)
        put = chosen(total.shape[1], col_where, lanes=128, offset=offset)
        half = sum(dot(gather, part) for part in split3(total))
        return sum(dot(part, put) for part in split3(half))

    packed = collapsed(g1[...], units(8), cells(48), 0)
    packed += collapsed(g2[...], units(), units(), 32)
    packed += collapsed(g3[...], units(), units(), 64)
    packed += collapsed(g4[...], cells(32), units(8), 96)
    for k in range(3):
        pick = (iota((HID, 128), 0) == 8 + k).astype(F32).astype(BF16)
        half = sum(dot(pick, part, 1, 1) for part in split3(gb[k]))
        put = chosen(HALF, units(), lanes=128, offset=96)
        packed += sum(dot(part, put) for part in split3(half))
    own_grad[...] = packed
    all_grads[me] = packed

    def grad_copy(i):
        return pltpu.make_async_remote_copy(
            src_ref=own_grad, dst_ref=all_grads.at[me],
            send_sem=grad_ss.at[i], recv_sem=grad_rs.at[me],
            device_id=device(peer(i)), device_id_type=pl.DeviceIdType.MESH,
        )

    def grad_arrival(i):
        return pltpu.make_async_remote_copy(
            src_ref=own_grad, dst_ref=all_grads.at[peer(i)],
            send_sem=grad_ss.at[i], recv_sem=grad_rs.at[peer(i)],
            device_id=device(peer(i)), device_id_type=pl.DeviceIdType.MESH,
        )

    @pl.loop(1, n)
    def _(i):
        grad_copy(i).start()

    @pl.loop(1, n)
    def _(i):
        grad_arrival(i).wait_recv()
        grad_copy(i).wait_send()

    grads[...] = jnp.sum(all_grads[...], axis=0) * (1.0 / math.sqrt(ROWS * cols * n))


def shards(
    state, bed_slope, terrain, wet_mask, state_cotangent, roughness,
    first_weight, second_weight, third_weight, output_weight, biases,
):
    nrow, ncol = lax.axis_size("row"), lax.axis_size("col")
    n = nrow * ncol
    cols = state.shape[2]
    assert state.shape[1] == ROWS
    params = jnp.concatenate(
        [
            jnp.pad(first_weight, ((0, 0), (0, HID - first_weight.shape[1]))),
            second_weight,
            third_weight,
            jnp.pad(output_weight, ((0, HID - output_weight.shape[0]), (0, 0))),
            jnp.pad(biases, ((0, 8 - biases.shape[0]), (0, 0))),
        ],
        axis=0,
    )
    vmem = pl.BlockSpec(memory_space=pltpu.VMEM)
    big = (WIDE, WIDE)
    final, adjoint, grads = pl.pallas_call(
        functools.partial(kernel, n, ncol, cols),
        out_shape=(
            jax.ShapeDtypeStruct((4 * ROWS, cols), F32),
            jax.ShapeDtypeStruct((4 * ROWS, cols), F32),
            jax.ShapeDtypeStruct((HID, 128), F32),
        ),
        in_specs=[vmem] * 6 + [pl.BlockSpec(memory_space=pltpu.SMEM)],
        out_specs=(vmem, vmem, vmem),
        scratch_shapes=[
            pltpu.VMEM((STEPS + 1, 4 * ROWS, cols), F32),
            pltpu.VMEM((4 * ROWS, cols), F32),
            pltpu.VMEM((4 * ROWS, cols), F32),
            pltpu.VMEM((4 * ROWS, cols), F32),
            pltpu.VMEM((ROWS, cols), F32),
            pltpu.VMEM((ROWS, cols), F32),
            pltpu.VMEM((STEPS, ROWS, 128), F32),
            pltpu.VMEM((WIDE, 144), BF16),
            pltpu.VMEM(big, BF16),
            pltpu.VMEM(big, BF16),
            pltpu.VMEM((64, 2 * WIDE), BF16),
            pltpu.VMEM(big, BF16),
            pltpu.VMEM(big, BF16),
            pltpu.VMEM((WIDE, 96), BF16),
            pltpu.VMEM((64, 2 * WIDE), BF16),
            pltpu.VMEM((3, HALF, 128), F32),
            pltpu.VMEM((KEPT, cols // CHUNK, 3, WIDE, 2 * CHUNK), BF16),
            pltpu.VMEM((2 * WIDE, 96), F32),
            pltpu.VMEM((WIDE, WIDE), F32),
            pltpu.VMEM((WIDE, WIDE), F32),
            pltpu.VMEM((64, 2 * WIDE), F32),
            pltpu.VMEM((3, HALF, 128), F32),
            pltpu.VMEM((STEPS, 2, 4, cols), F32),
            pltpu.VMEM((STEPS, 2, 4, cols), F32),
            pltpu.VMEM((STEPS, 2, 4, cols), F32),
            pltpu.VMEM((STEPS, 2, 4, cols), F32),
            pltpu.VMEM((STEPS, ROWS, 128), F32),
            pltpu.VMEM((STEPS, n, ROWS, 128), F32),
            pltpu.VMEM((HID, 128), F32),
            pltpu.VMEM((n, HID, 128), F32),
            pltpu.SemaphoreType.DMA((2 * STEPS, 2)),
            pltpu.SemaphoreType.DMA((2 * STEPS, 2)),
            pltpu.SemaphoreType.DMA((n,)),
            pltpu.SemaphoreType.DMA((STEPS, n)),
            pltpu.SemaphoreType.DMA((n,)),
            pltpu.SemaphoreType.DMA((n,)),
        ],
        compiler_params=pltpu.CompilerParams(
            collective_id=0, has_side_effects=True, vmem_limit_bytes=62 * 1024 * 1024
        ),
    )(
        state.reshape(4 * ROWS, cols),
        bed_slope.reshape(2 * ROWS, cols),
        terrain,
        wet_mask,
        state_cotangent.reshape(4 * ROWS, cols),
        params,
        roughness,
    )
    feat, outs, layers = first_weight.shape[1], output_weight.shape[0], biases.shape[0]
    return (
        final.reshape(state.shape),
        adjoint.reshape(state.shape),
        grads[:, 0:feat],
        grads[:, 32:64],
        grads[:, 64:96],
        grads[0:outs, 96:128],
        grads[8 : 8 + layers, 96:128],
    )


def solution(mesh):
    grid = P(None, ("grp", "row", "col"), None)
    flat = P(("grp", "row", "col"), None)
    in_specs = (grid, grid, flat, flat, grid, P(), P(), P(), P(), P(), P())
    out_specs = (grid, grid) + (P("grp", None),) * 5
    return jax.shard_map(shards, mesh=mesh, in_specs=in_specs, out_specs=out_specs, check_vma=False)
```
